32 devices in a mesh: seq: 8 (over y, x, core), head: 4 (over z).
Axes of the slice: x: 2, y: 2, z: 4, core: 2. Of those that a mesh axis runs over, the one named last changes fastest.
Arguments:
- queries: bfloat16 [1024, 8192], P('seq', 'head'), may hold values from -24 to 24
- key_rows: bfloat16 [1024, 1024], P('seq', 'head'), may hold values from -6 to 6
- value_rows: bfloat16 [1024, 1024], P('seq', 'head'), may hold values from -6 to 6
- out_weight: bfloat16 [8192, 8192], P('head'), may hold values from -0.5 to 0.5
- residual: bfloat16 [1024, 8192], P('seq', 'head'), may hold values from -54 to 54
- norm_gain: float32 [8192], replicated, may hold values from 0.1 to 1.9
- gate_weight: bfloat16 [8192, 28672], P(None, ('seq', 'head')), may hold values from -0.0625 to 0.0625
- up_weight: bfloat16 [8192, 28672], P(None, ('seq', 'head')), may hold values from -0.0625 to 0.0625
Outputs:
- edit_keys: bfloat16 [1024, 28672], P(None, ('seq', 'head'))
- hidden_state: bfloat16 [1024, 8192], P('seq', 'head')
The draws below stay inside these ranges and needn't reach their ends.
All inputs are finite; a program needn't handle non-finite values.
Results may differ from the reference program's by a relative error of at most 0.019.
Values may be sent and summed in bfloat16 or wider, within the bound.
A program may use at most 128 MiB of HBM per device.

```python
import math
import jax
import jax.numpy as jnp
from jax import lax

D = 8192
QH = 64
KVH = 8
HD = 128
FF = 28672
TOKENS = 1024


def attention_draw(key):
    base_key = jax.random.fold_in(key, 17)
    query_key, keys_key = jax.random.split(base_key, 2)
    query_vals = jnp.clip(1.5 * jax.random.normal(query_key, (TOKENS, QH * HD), jnp.float32), -9.0, 9.0)
    key_vals = jnp.clip(jax.random.normal(keys_key, (TOKENS, KVH * HD), jnp.float32), -6.0, 6.0)
    return (query_vals, key_vals)


def draw_queries(key, part):
    return attention_draw(key)[0].astype(jnp.bfloat16)


def draw_key_rows(key, part):
    return attention_draw(key)[1].astype(jnp.bfloat16)


def draw_residual(key, part):
    base_key = jax.random.fold_in(key, 29)
    row_key, column_key, value_key = jax.random.split(base_key, 3)
    row_scale = jnp.exp(jax.random.uniform(row_key, (TOKENS, 1), jnp.float32, math.log(0.3), math.log(3.0)))
    ramp = 0.5 + jnp.arange(D, dtype=jnp.float32)[None, :] / D
    column_scale = ramp * jnp.exp(jax.random.uniform(column_key, (1, D), jnp.float32, math.log(0.3), math.log(3.0)))
    values = jnp.clip(jax.random.normal(value_key, (TOKENS, D), jnp.float32), -4.0, 4.0)
    return (values * row_scale * column_scale).astype(jnp.bfloat16)


def strengthened(entries, key, source, target, parts, factor):
    def block_of(dim):
        return (jnp.arange(entries.shape[dim]) // (entries.shape[dim] // parts)).reshape((-1,) + (1,) * (entries.ndim - 1 - dim))

    near = jax.random.permutation(key, parts)[block_of(target)]
    other_side = (block_of(target) + parts // 2) % parts
    return jnp.where((block_of(source) == near) | (block_of(source) == other_side), factor * entries, entries)


def shard_levels(stream_key, extent, pieces, low, high):
    gain, own = 1.0, jax.random.fold_in(stream_key, 6)
    for dim, shards_of in pieces:
        heights = jnp.exp(jax.random.uniform(jax.random.fold_in(own, dim), (shards_of,), jnp.float32, low / len(pieces), high / len(pieces)))
        gain = gain * jnp.repeat(heights, extent[dim] // shards_of).reshape([-1 if axis == dim else 1 for axis in range(len(extent))])
    return gain


def bell_draw(own_key, shape, spread, most, shards=(), kind=jnp.bfloat16):
    entries = jax.random.normal(own_key, shape, jnp.float32) * spread
    if len(shards) > 0:
        entries = shard_levels(own_key, shape, shards, -0.22, 0.18) * entries
    return jnp.clip(entries, min=-most, max=most).astype(kind)


def bell_draw_with(rng, extent, deviation, bound, pieces, heavy, kind=jnp.bfloat16):
    drawn = deviation * jax.random.normal(rng, extent, jnp.float32)
    if pieces:
        drawn = drawn * shard_levels(rng, extent, pieces, -0.22, 0.18)
    return jnp.clip(strengthened(drawn, jax.random.fold_in(rng, 3), *heavy), -bound, bound).astype(kind)


def setup_inputs(seed: int = 0) -> dict:
    keys = jax.random.split(jax.random.key(seed), 9)
    return {
        "queries": draw_queries(jax.random.fold_in(keys[8], 71), 0),
        "key_rows": draw_key_rows(jax.random.fold_in(keys[8], 71), 0),
        "value_rows": bell_draw(keys[2], (TOKENS, KVH * HD), 1.0, 6.0, ((0, 8), (1, 4))),
        "out_weight": bell_draw_with(keys[3], (QH * HD, D), (2 * HD) ** -0.5, 0.5, ((0, 4),), (0, 1, 4, 2.0)),
        "residual": draw_residual(jax.random.fold_in(keys[8], 71), 0),
        "norm_gain": jnp.clip(1.0 + 0.18 * jax.random.normal(keys[5], (D,), jnp.float32), 0.1, 1.9),
        "gate_weight": bell_draw(keys[6], (D, FF), D ** -0.5, 0.0625, ((1, 32),)),
        "up_weight": bell_draw(keys[7], (D, FF), D ** -0.5, 0.0625, ((1, 32),)),
    }


very_low = -1e+30

def group_attend(group_item):
    group_queries, group_keys, group_values = group_item
    length = group_queries.shape[1]
    scores = jnp.einsum('gqd,kd->gqk', group_queries.astype(jnp.float32), group_keys.astype(jnp.float32), precision=lax.Precision.HIGHEST) / jnp.sqrt(jnp.float32(HD))
    query_places = jnp.arange(length, dtype=jnp.int32)
    visible = query_places[:, None] >= query_places[None, :]
    scores = jnp.where(visible[None], scores, jnp.float32(very_low))
    maxima = lax.optimization_barrier(jnp.max(scores, axis=-1, keepdims=True))
    weights = jnp.exp(scores - maxima)
    totals = lax.optimization_barrier(jnp.sum(weights, axis=-1))
    summed = jnp.einsum('gqk,kd->gqd', weights, group_values.astype(jnp.float32), precision=lax.Precision.HIGHEST)
    return summed / totals[..., None]

def reference(queries, key_rows, value_rows, out_weight, residual, norm_gain, gate_weight, up_weight):
    length = queries.shape[0]
    group_size = QH // KVH
    query_groups = queries.reshape(length, KVH, group_size, HD).transpose(1, 2, 0, 3)
    key_groups = key_rows.reshape(length, KVH, HD).transpose(1, 0, 2)
    value_groups = value_rows.reshape(length, KVH, HD).transpose(1, 0, 2)
    results = lax.map(group_attend, (query_groups, key_groups, value_groups))
    attended = results.transpose(2, 0, 1, 3).reshape(length, QH * HD).astype(jnp.bfloat16)
    projected = jnp.dot(attended, out_weight, preferred_element_type=jnp.float32)
    hidden_state = (residual.astype(jnp.float32) + projected).astype(jnp.bfloat16)
    widened = hidden_state.astype(jnp.float32)
    mean_square = lax.optimization_barrier(jnp.sum(widened * widened, axis=-1, keepdims=True)) / D
    normed = (widened * lax.rsqrt(mean_square + 1e-05) * norm_gain[None, :]).astype(jnp.bfloat16)
    gate_sums = jnp.dot(normed, gate_weight, preferred_element_type=jnp.float32)
    up_sums = jnp.dot(normed, up_weight, preferred_element_type=jnp.float32)
    edit_keys = (jax.nn.silu(gate_sums) * up_sums).astype(jnp.bfloat16)
    return (edit_keys, hidden_state)
```

```python
import functools
import jax
import jax.numpy as jnp
from jax import lax
from jax.experimental import pallas as pl
from jax.experimental.pallas import tpu as pltpu
from jax.sharding import PartitionSpec as P

HD = 128
MESH = pl.DeviceIdType.MESH
VMEM_LIMIT = 60 * 1024 * 1024


very_low = -1e30


def chip_at(place):
    return (place // 2) * 2 + (place % 2 + place // 2) % 2


def gather_kernel(
    n_s, n_h, x_in, gate_hbm, up_hbm, out_ref,
    x, gate_w, up_w, acc, net_sem, sib_sem, send_sem, weight_sem,
):
    seq = lax.axis_index("seq")
    z = lax.axis_index("head")
    rows, cols = x_in.shape
    hidden = gate_hbm.shape[1]
    n_c = n_s // 2
    half = n_c // 2
    core = seq % 2
    chip = seq // 2
    sibling = chip * 2 + 1 - core
    place = chip_at(chip)
    right = chip_at((place + 1) % n_c) * 2 + core
    left = chip_at((place + n_c - 1) % n_c) * 2 + core
    has_up = z + 1 < n_h
    has_down = z > 0
    short = jnp.minimum(z, n_h - 1 - z)

    def part_of(rank):
        near = z + ((rank + 1) // 2) * (1 - 2 * (rank % 2))
        far = jnp.where(z == short, rank, n_h - 1 - rank)
        return jnp.where(rank <= 2 * short, near, far)

    barrier = pltpu.get_barrier_semaphore()
    for other in (sibling, right, left):
        pl.semaphore_signal(barrier, inc=1, device_id=(other, z), device_id_type=MESH)

    @pl.when(has_up)
    def _():
        pl.semaphore_signal(barrier, inc=1, device_id=(seq, z + 1), device_id_type=MESH)

    @pl.when(has_down)
    def _():
        pl.semaphore_signal(barrier, inc=1, device_id=(seq, z - 1), device_id_type=MESH)

    def weight_copies(part):
        depth = pl.ds(pl.multiple_of(part * cols, cols), cols)
        return (
            pltpu.make_async_copy(gate_hbm.at[depth], gate_w.at[depth], weight_sem.at[0, part]),
            pltpu.make_async_copy(up_hbm.at[depth], up_w.at[depth], weight_sem.at[1, part]),
        )

    @pl.loop(0, n_h)
    def _(rank):
        for copy in weight_copies(part_of(rank)):
            copy.start()

    def block(source, owner_core, part):
        first = pl.multiple_of((source * 2 + owner_core) * rows, rows)
        return x.at[part, pl.ds(first, rows), :]

    def to(way, source, part, target, sems):
        held = block(source, core, part)
        return pltpu.make_async_remote_copy(
            src_ref=held,
            dst_ref=held,
            send_sem=send_sem.at[way, source, part],
            recv_sem=sems.at[source, part],
            device_id=target,
            device_id_type=MESH,
        )

    def unit(step, turn):
        distance = (turn + 1) // 2
        rank = step - distance
        valid = jnp.logical_and(rank >= 0, rank < n_h)
        safe = jnp.clip(rank, 0, n_h - 1)
        part = part_of(safe)
        source = chip_at((place + n_c + distance * (1 - 2 * (turn % 2))) % n_c)
        return distance, rank, valid, part, source

    def sends(step, turn, act):
        distance, rank, valid, part, source = unit(step, turn)
        own = turn == 0
        last_right = part % 2 == 0
        onward = distance + 1
        from_left = turn % 2 == 1
        more_right = jnp.logical_or(onward < half, jnp.logical_and(onward == half, last_right))
        more_left = jnp.logical_or(
            onward < half, jnp.logical_and(onward == half, jnp.logical_not(last_right))
        )
        go_right = jnp.logical_or(own, jnp.logical_and(from_left, more_right))
        go_left = jnp.logical_or(own, jnp.logical_and(jnp.logical_not(from_left), more_left))
        go_up = jnp.logical_and(own, jnp.logical_and(part <= z, has_up))
        go_down = jnp.logical_and(own, jnp.logical_and(part >= z, has_down))

        @pl.when(jnp.logical_and(valid, go_up))
        def _():
            act(to(0, source, part, (seq, z + 1), net_sem))

        @pl.when(jnp.logical_and(valid, go_down))
        def _():
            act(to(1, source, part, (seq, z - 1), net_sem))

        @pl.when(jnp.logical_and(valid, go_right))
        def _():
            act(to(2, source, part, (right, z), net_sem))

        @pl.when(jnp.logical_and(valid, go_left))
        def _():
            act(to(3, source, part, (left, z), net_sem))

        @pl.when(valid)
        def _():
            act(to(4, source, part, (sibling, z), sib_sem))

    first = pl.multiple_of(seq * rows, rows)
    x[z, pl.ds(first, rows), :] = x_in[...]
    neighbours = 3 + has_up.astype(jnp.int32) + has_down.astype(jnp.int32)
    pl.semaphore_wait(barrier, neighbours)

    steps = n_h + half

    @pl.loop(0, steps)
    def _(step):
        @pl.loop(0, n_c)
        def _(turn):
            distance, rank, valid, part, source = unit(step, turn)

            @pl.when(jnp.logical_and(valid, step > 0))
            def _():
                to(2, source, part, (right, z), net_sem).wait_recv()

            sends(step, turn, lambda copy: copy.start())

        @pl.loop(0, n_c)
        def _(turn):
            distance, rank, valid, part, source = unit(step, turn)

            @pl.when(jnp.logical_and(valid, turn == 0))
            def _():
                for copy in weight_copies(part):
                    copy.wait()

            @pl.when(valid)
            def _():
                other = block(source, 1 - core, part)
                pltpu.make_async_remote_copy(
                    src_ref=other,
                    dst_ref=other,
                    send_sem=send_sem.at[4, source, part],
                    recv_sem=sib_sem.at[source, part],
                    device_id=(sibling, z),
                    device_id_type=MESH,
                ).wait_recv()
                start = pl.multiple_of(source * 2 * rows, 2 * rows)
                here = pl.ds(start, 2 * rows)
                depth = pl.ds(pl.multiple_of(part * cols, cols), cols)
                features = x[part, here, :]
                gate = jnp.dot(features, gate_w[depth, :], preferred_element_type=jnp.float32)

                @pl.when(rank == 0)
                def _():
                    acc[0, here, :] = gate

                @pl.when(rank > 0)
                def _():
                    acc[0, here, :] += gate

                up = jnp.dot(features, up_w[depth, :], preferred_element_type=jnp.float32)

                @pl.when(rank == 0)
                def _():
                    acc[1, here, :] = up

                @pl.when(rank > 0)
                def _():
                    acc[1, here, :] += up

            @pl.when(rank == n_h - 1)
            def _():
                start = pl.multiple_of(source * 2 * rows, 2 * rows)
                here = pl.ds(start, 2 * rows)
                gate = acc[0, here, :]
                out_ref[here, :] = (gate / (1.0 + jnp.exp(-gate)) * acc[1, here, :]).astype(
                    out_ref.dtype
                )

    @pl.loop(0, steps)
    def _(step):
        @pl.loop(0, n_c)
        def _(turn):
            sends(step, turn, lambda copy: copy.wait_send())


def gathered_keys(n_s, n_h, normed, gate_weight, up_weight):
    rows, cols = normed.shape
    tokens = n_s * rows
    width, hidden = gate_weight.shape
    n_c = n_s // 2
    return pl.pallas_call(
        functools.partial(gather_kernel, n_s, n_h),
        out_shape=jax.ShapeDtypeStruct((tokens, hidden), jnp.bfloat16),
        in_specs=[
            pl.BlockSpec(memory_space=pltpu.VMEM),
            pl.BlockSpec(memory_space=pl.ANY),
            pl.BlockSpec(memory_space=pl.ANY),
        ],
        out_specs=pl.BlockSpec(memory_space=pltpu.VMEM),
        scratch_shapes=[
            pltpu.VMEM((n_h, tokens, cols), jnp.bfloat16),
            pltpu.VMEM((width, hidden), jnp.bfloat16),
            pltpu.VMEM((width, hidden), jnp.bfloat16),
            pltpu.VMEM((2, tokens, hidden), jnp.float32),
            pltpu.SemaphoreType.DMA((n_c, n_h)),
            pltpu.SemaphoreType.DMA((n_c, n_h)),
            pltpu.SemaphoreType.DMA((5, n_c, n_h)),
            pltpu.SemaphoreType.DMA((2, n_h)),
        ],
        compiler_params=pltpu.CompilerParams(
            collective_id=0, has_side_effects=True, vmem_limit_bytes=VMEM_LIMIT
        ),
        cost_estimate=pl.CostEstimate(
            flops=4 * tokens * width * hidden,
            bytes_accessed=4 * width * hidden,
            transcendentals=tokens * hidden,
        ),
        name="gather_and_project",
    )(normed, gate_weight, up_weight)


def attend(rows, places, key_piece, value_piece, key_places):
    scores = jnp.einsum(
        "rkgd,nkd->kgrn", rows, key_piece, preferred_element_type=jnp.float32
    ) / jnp.sqrt(jnp.float32(HD))
    visible = places[:, None] >= key_places[None, :]
    scores = jnp.where(visible, scores, jnp.float32(very_low))
    maxima = jnp.max(scores, axis=-1)
    weights = jnp.exp(scores - maxima[..., None])
    totals = jnp.sum(weights, axis=-1)
    products = jnp.einsum(
        "kgrn,nkd->kgrd", weights, value_piece.astype(jnp.float32), precision=lax.Precision.HIGHEST
    )
    result = products / totals[..., None]
    row_count = rows.shape[0]
    return result.transpose(2, 0, 1, 3).reshape(row_count, -1).astype(jnp.bfloat16)


def per_device(
    n_s, n_h, queries, key_rows, value_rows, out_weight, residual, norm_gain, gate_weight, up_weight
):
    tok_count = queries.shape[0]
    seq_index = lax.axis_index("seq")
    head_index = lax.axis_index("head")
    kv_local = key_rows.shape[1] // HD
    q_local = queries.shape[1] // HD
    group_size = q_local // kv_local
    places = seq_index * tok_count + jnp.arange(tok_count, dtype=jnp.int32)
    both = lax.all_gather(
        jnp.concatenate([key_rows, value_rows], axis=1), "seq", axis=0, tiled=True
    )
    width = key_rows.shape[1]
    key_piece = both[:, :width].reshape(-1, kv_local, HD)
    value_piece = both[:, width:].reshape(-1, kv_local, HD)
    key_places = jnp.arange(key_piece.shape[0], dtype=jnp.int32)
    attended = attend(
        queries.reshape(tok_count, kv_local, group_size, HD),
        places, key_piece, value_piece, key_places,
    )
    projected = jnp.dot(attended, out_weight, preferred_element_type=jnp.float32)
    width_total = out_weight.shape[1]
    width_local = residual.shape[1]
    column_first = head_index * width_local
    summed = lax.psum_scatter(
        projected.astype(jnp.bfloat16), "head", scatter_dimension=1, tiled=True
    )
    hidden_state = (summed.astype(jnp.float32) + residual.astype(jnp.float32)).astype(jnp.bfloat16)
    widened = hidden_state.astype(jnp.float32)
    mean_square = (
        lax.psum(jnp.sum(widened * widened, axis=-1, keepdims=True), "head") / width_total
    )
    gain = lax.dynamic_slice_in_dim(norm_gain, column_first, width_local, 0)
    normed = (widened * lax.rsqrt(mean_square + 1e-05) * gain[None, :]).astype(jnp.bfloat16)
    edit_keys = gathered_keys(n_s, n_h, normed, gate_weight, up_weight)
    return (edit_keys, hidden_state)


def solution(mesh):
    return jax.shard_map(
        functools.partial(per_device, mesh.shape["seq"], mesh.shape["head"]),
        mesh=mesh,
        in_specs=(
            P("seq", "head"),
            P("seq", "head"),
            P("seq", "head"),
            P("head", None),
            P("seq", "head"),
            P(),
            P(None, ("seq", "head")),
            P(None, ("seq", "head")),
        ),
        out_specs=(P(None, ("seq", "head")), P("seq", "head")),
        check_vma=False,
    )
```

```python
import functools
import jax
import jax.numpy as jnp
from jax import lax
from jax.experimental import pallas as pl
from jax.experimental.pallas import tpu as pltpu
from jax.sharding import PartitionSpec as P

HD = 128
MESH = pl.DeviceIdType.MESH
VMEM_LIMIT = 60 * 1024 * 1024


very_low = -1e30


def chip_at(place):
    return (place // 2) * 2 + (place % 2 + place // 2) % 2


def gather_kernel(
    n_s, n_h, x_in, gate_hbm, up_hbm, out_ref,
    x, gate_w, up_w, acc, net_sem, sib_sem, send_sem, weight_sem,
):
    seq = lax.axis_index("seq")
    z = lax.axis_index("head")
    rows, cols = x_in.shape
    hidden = gate_hbm.shape[1]
    n_c = n_s // 2
    half = n_c // 2
    core = seq % 2
    chip = seq // 2
    sibling = chip * 2 + 1 - core
    place = chip_at(chip)
    right = chip_at((place + 1) % n_c) * 2 + core
    left = chip_at((place + n_c - 1) % n_c) * 2 + core
    has_up = z + 1 < n_h
    has_down = z > 0
    short = jnp.minimum(z, n_h - 1 - z)

    def part_of(rank):
        near = z + ((rank + 1) // 2) * (1 - 2 * (rank % 2))
        far = jnp.where(z == short, rank, n_h - 1 - rank)
        return jnp.where(rank <= 2 * short, near, far)

    barrier = pltpu.get_barrier_semaphore()
    for other in (sibling, right, left):
        pl.semaphore_signal(barrier, inc=1, device_id=(other, z), device_id_type=MESH)

    @pl.when(has_up)
    def _():
        pl.semaphore_signal(barrier, inc=1, device_id=(seq, z + 1), device_id_type=MESH)

    @pl.when(has_down)
    def _():
        pl.semaphore_signal(barrier, inc=1, device_id=(seq, z - 1), device_id_type=MESH)

    def weight_copies(part):
        depth = pl.ds(pl.multiple_of(part * cols, cols), cols)
        return (
            pltpu.make_async_copy(gate_hbm.at[depth], gate_w.at[depth], weight_sem.at[0, part]),
            pltpu.make_async_copy(up_hbm.at[depth], up_w.at[depth], weight_sem.at[1, part]),
        )

    @pl.loop(0, n_h)
    def _(rank):
        for copy in weight_copies(part_of(rank)):
            copy.start()

    def block(source, owner_core, part):
        first = pl.multiple_of((source * 2 + owner_core) * rows, rows)
        return x.at[part, pl.ds(first, rows), :]

    def to(way, source, part, target, sems):
        held = block(source, core, part)
        return pltpu.make_async_remote_copy(
            src_ref=held,
            dst_ref=held,
            send_sem=send_sem.at[way, source, part],
            recv_sem=sems.at[source, part],
            device_id=target,
            device_id_type=MESH,
        )

    def unit(step, turn):
        distance = (turn + 1) // 2
        rank = step - distance
        valid = jnp.logical_and(rank >= 0, rank < n_h)
        safe = jnp.clip(rank, 0, n_h - 1)
        part = part_of(safe)
        source = chip_at((place + n_c + distance * (1 - 2 * (turn % 2))) % n_c)
        return distance, rank, valid, part, source

    def sends(step, turn, act):
        distance, rank, valid, part, source = unit(step, turn)
        own = turn == 0
        last_right = part % 2 == 0
        onward = distance + 1
        from_left = turn % 2 == 1
        more_right = jnp.logical_or(onward < half, jnp.logical_and(onward == half, last_right))
        more_left = jnp.logical_or(
            onward < half, jnp.logical_and(onward == half, jnp.logical_not(last_right))
        )
        go_right = jnp.logical_or(own, jnp.logical_and(from_left, more_right))
        go_left = jnp.logical_or(own, jnp.logical_and(jnp.logical_not(from_left), more_left))
        go_up = jnp.logical_and(own, jnp.logical_and(part <= z, has_up))
        go_down = jnp.logical_and(own, jnp.logical_and(part >= z, has_down))

        @pl.when(jnp.logical_and(valid, go_up))
        def _():
            act(to(0, source, part, (seq, z + 1), net_sem))

        @pl.when(jnp.logical_and(valid, go_down))
        def _():
            act(to(1, source, part, (seq, z - 1), net_sem))

        @pl.when(jnp.logical_and(valid, go_right))
        def _():
            act(to(2, source, part, (right, z), net_sem))

        @pl.when(jnp.logical_and(valid, go_left))
        def _():
            act(to(3, source, part, (left, z), net_sem))

        @pl.when(valid)
        def _():
            act(to(4, source, part, (sibling, z), sib_sem))

    first = pl.multiple_of(seq * rows, rows)
    x[z, pl.ds(first, rows), :] = x_in[...]
    neighbours = 3 + has_up.astype(jnp.int32) + has_down.astype(jnp.int32)
    pl.semaphore_wait(barrier, neighbours)

    steps = n_h + half

    @pl.loop(0, steps)
    def _(step):
        @pl.loop(0, n_c)
        def _(turn):
            distance, rank, valid, part, source = unit(step, turn)

            @pl.when(jnp.logical_and(valid, step > 0))
            def _():
                to(2, source, part, (right, z), net_sem).wait_recv()

            sends(step, turn, lambda copy: copy.start())

        @pl.loop(0, n_c)
        def _(turn):
            distance, rank, valid, part, source = unit(step, turn)

            @pl.when(jnp.logical_and(valid, turn == 0))
            def _():
                for copy in weight_copies(part):
                    copy.wait()

            @pl.when(valid)
            def _():
                other = block(source, 1 - core, part)
                pltpu.make_async_remote_copy(
                    src_ref=other,
                    dst_ref=other,
                    send_sem=send_sem.at[4, source, part],
                    recv_sem=sib_sem.at[source, part],
                    device_id=(sibling, z),
                    device_id_type=MESH,
                ).wait_recv()
                start = pl.multiple_of(source * 2 * rows, 2 * rows)
                here = pl.ds(start, 2 * rows)
                depth = pl.ds(pl.multiple_of(part * cols, cols), cols)
                features = x[part, here, :]
                gate = jnp.dot(features, gate_w[depth, :], preferred_element_type=jnp.float32)

                @pl.when(rank == 0)
                def _():
                    acc[0, here, :] = gate

                @pl.when(rank > 0)
                def _():
                    acc[0, here, :] += gate

                up = jnp.dot(features, up_w[depth, :], preferred_element_type=jnp.float32)

                @pl.when(rank == 0)
                def _():
                    acc[1, here, :] = up

                @pl.when(rank > 0)
                def _():
                    acc[1, here, :] += up

            @pl.when(rank == n_h - 1)
            def _():
                start = pl.multiple_of(source * 2 * rows, 2 * rows)
                here = pl.ds(start, 2 * rows)
                gate = acc[0, here, :]
                out_ref[here, :] = (gate / (1.0 + jnp.exp(-gate)) * acc[1, here, :]).astype(
                    out_ref.dtype
                )

    @pl.loop(0, steps)
    def _(step):
        @pl.loop(0, n_c)
        def _(turn):
            sends(step, turn, lambda copy: copy.wait_send())


def gathered_keys(n_s, n_h, normed, gate_weight, up_weight):
    rows, cols = normed.shape
    tokens = n_s * rows
    width, hidden = gate_weight.shape
    n_c = n_s // 2
    return pl.pallas_call(
        functools.partial(gather_kernel, n_s, n_h),
        out_shape=jax.ShapeDtypeStruct((tokens, hidden), jnp.bfloat16),
        in_specs=[
            pl.BlockSpec(memory_space=pltpu.VMEM),
            pl.BlockSpec(memory_space=pl.ANY),
            pl.BlockSpec(memory_space=pl.ANY),
        ],
        out_specs=pl.BlockSpec(memory_space=pltpu.VMEM),
        scratch_shapes=[
            pltpu.VMEM((n_h, tokens, cols), jnp.bfloat16),
            pltpu.VMEM((width, hidden), jnp.bfloat16),
            pltpu.VMEM((width, hidden), jnp.bfloat16),
            pltpu.VMEM((2, tokens, hidden), jnp.float32),
            pltpu.SemaphoreType.DMA((n_c, n_h)),
            pltpu.SemaphoreType.DMA((n_c, n_h)),
            pltpu.SemaphoreType.DMA((5, n_c, n_h)),
            pltpu.SemaphoreType.DMA((2, n_h)),
        ],
        compiler_params=pltpu.CompilerParams(
            collective_id=0, has_side_effects=True, vmem_limit_bytes=VMEM_LIMIT
        ),
        cost_estimate=pl.CostEstimate(
            flops=4 * tokens * width * hidden,
            bytes_accessed=4 * width * hidden,
            transcendentals=tokens * hidden,
        ),
        name="gather_and_project",
    )(normed, gate_weight, up_weight)


def attend(rows, places, key_piece, value_piece, key_places):
    scores = jnp.einsum(
        "rkgd,nkd->kgrn", rows, key_piece, preferred_element_type=jnp.float32
    ) / jnp.sqrt(jnp.float32(HD))
    visible = places[:, None] >= key_places[None, :]
    scores = jnp.where(visible, scores, jnp.float32(very_low))
    maxima = jnp.max(scores, axis=-1)
    weights = jnp.exp(scores - maxima[..., None])
    totals = jnp.sum(weights, axis=-1)
    products = jnp.einsum(
        "kgrn,nkd->kgrd",
        weights.astype(jnp.bfloat16),
        value_piece,
        preferred_element_type=jnp.float32,
    )
    result = products / totals[..., None]
    row_count = rows.shape[0]
    return result.transpose(2, 0, 1, 3).reshape(row_count, -1).astype(jnp.bfloat16)


def per_device(
    n_s, n_h, queries, key_rows, value_rows, out_weight, residual, norm_gain, gate_weight, up_weight
):
    tok_count = queries.shape[0]
    seq_index = lax.axis_index("seq")
    head_index = lax.axis_index("head")
    kv_local = key_rows.shape[1] // HD
    q_local = queries.shape[1] // HD
    group_size = q_local // kv_local
    places = seq_index * tok_count + jnp.arange(tok_count, dtype=jnp.int32)
    key_piece = lax.all_gather(key_rows, "seq", axis=0, tiled=True).reshape(-1, kv_local, HD)
    value_piece = lax.all_gather(value_rows, "seq", axis=0, tiled=True).reshape(-1, kv_local, HD)
    key_places = jnp.arange(key_piece.shape[0], dtype=jnp.int32)
    attended = attend(
        queries.reshape(tok_count, kv_local, group_size, HD),
        places, key_piece, value_piece, key_places,
    )
    projected = jnp.dot(attended, out_weight, preferred_element_type=jnp.float32)
    width_total = out_weight.shape[1]
    width_local = residual.shape[1]
    column_first = head_index * width_local
    summed = lax.psum_scatter(
        projected.astype(jnp.bfloat16), "head", scatter_dimension=1, tiled=True
    )
    hidden_state = (summed.astype(jnp.float32) + residual.astype(jnp.float32)).astype(jnp.bfloat16)
    widened = hidden_state.astype(jnp.float32)
    mean_square = (lax.psum(jnp.sum(widened * widened, axis=-1), "head") / width_total)[:, None]
    gain = lax.dynamic_slice_in_dim(norm_gain, column_first, width_local, 0)
    normed = (widened * lax.rsqrt(mean_square + 1e-05) * gain[None, :]).astype(jnp.bfloat16)
    edit_keys = gathered_keys(n_s, n_h, normed, gate_weight, up_weight)
    return (edit_keys, hidden_state)


def solution(mesh):
    return jax.shard_map(
        functools.partial(per_device, mesh.shape["seq"], mesh.shape["head"]),
        mesh=mesh,
        in_specs=(
            P("seq", "head"),
            P("seq", "head"),
            P("seq", "head"),
            P("head", None),
            P("seq", "head"),
            P(),
            P(None, ("seq", "head")),
            P(None, ("seq", "head")),
        ),
        out_specs=(P(None, ("seq", "head")), P("seq", "head")),
        check_vma=False,
    )
```
